256 devices in a mesh: lon: 16 (over z, y_lo), lat: 16 (over x, y_hi, core).
Axes of the slice: x: 4, y: 4 (y_hi: 2, y_lo: 2; y = y_hi * 2 + y_lo), z: 8, core: 2. Of those that a mesh axis runs over, the one named last changes fastest.
Arguments:
- latent: bfloat16 [256, 1024, 256], P('lat', 'lon'), may hold values from -6 to 6
- w_first: bfloat16 [3, 3, 256, 256], replicated, may hold values from -0.125 to 0.125
- w_second: bfloat16 [3, 3, 256, 256], replicated, may hold values from -0.125 to 0.125
- levels: int32 [256], replicated, may hold values from 3 to 9, as said below
- prior_scale: float32 [256], replicated, may hold values from 0.5 to 3
- bins: int32 [256, 1024, 256], P('lat', 'lon'), may hold values from 0 to 8, as said below
- code_grad: bfloat16 [256, 1024, 256], P('lat', 'lon'), may hold values from -6 to 6
Outputs:
- grad_latent: float32 [256, 1024, 256], P('lat', 'lon')
- grad_first: float32 [2304, 256], P('lon', 'lat')
- grad_second: float32 [2304, 256], P('lon', 'lat')
The draws below stay inside these ranges and needn't reach their ends.
Inputs may be any that keep to these rules, and one draw needn't show every extreme that they name: `levels`: every level count is odd; each of 3, 5, 7 and 9 is held by a quarter of the channels. `bins`: each entry lies between 0 and its channel's level count minus 1.
All inputs are finite; a program needn't handle non-finite values.
Results may differ from the reference program's by a relative error of at most 0.0046.
Values may be sent and summed in bfloat16 or wider, within the bound.
No kernel may reach another device: no remote copies, remote signals or barrier semaphores. Data moves between devices by JAX's collectives and lax.ppermute only.
A program may use at most 64 MiB of HBM per device.

```python
import math
import jax
import jax.numpy as jnp
from jax import lax

C = 256
NLAT = 256
NLON = 1024


def shared_levels(key):
    ordering = jax.random.permutation(jax.random.fold_in(key, 11), C)
    return (3 + 2 * (ordering % 4)).astype(jnp.int32)


def draw_levels(key, part):
    return shared_levels(key)


def draw_bins(key, part):
    level_counts = shared_levels(key)
    key = jax.random.fold_in(key, 5)
    values = jax.random.randint(key, (NLAT, NLON, C), 0, level_counts)
    values = values.at[0, 0].set(level_counts - 1)
    values = values.at[0, 1].set(0)
    return values.astype(jnp.int32)


def raised(result, key, source, target, blocks, factor):
    def block_of(axis_at):
        return (jnp.arange(result.shape[axis_at]) // (result.shape[axis_at] // blocks)).reshape((-1,) + (1,) * (result.ndim - 1 - axis_at))

    first = jax.random.permutation(key, blocks)[block_of(target)]
    other_side = (block_of(target) + blocks // 2) % blocks
    return jnp.where((block_of(source) == first) | (block_of(source) == other_side), factor * result, result)


def block_levels(key, extent, shards, low, high):
    gain, own = 1.0, jax.random.fold_in(key, 6)
    for axis_at, blocks in shards:
        steps = jnp.exp(jax.random.uniform(jax.random.fold_in(own, axis_at), (blocks,), jnp.float32, low / len(shards), high / len(shards)))
        gain = gain * jnp.repeat(steps, extent[axis_at] // blocks).reshape([-1 if axis == axis_at else 1 for axis in range(len(extent))])
    return gain


def bell_draw(stream_key, shape, deviation, limit, shards=(), dtype=jnp.bfloat16):
    array = jax.random.normal(stream_key, shape, jnp.float32) * deviation
    if len(shards) > 0:
        array = block_levels(stream_key, shape, shards, -0.22, 0.18) * array
    return jnp.clip(array, min=-limit, max=limit).astype(dtype)


def heavy_noise(stream_key, extent, scale, bound, shards, heavy, kind=jnp.bfloat16):
    result = scale * jax.random.normal(stream_key, extent, jnp.float32)
    if shards:
        result = result * block_levels(stream_key, extent, shards, -0.22, 0.18)
    return jnp.clip(raised(result, jax.random.fold_in(stream_key, 3), *heavy), -bound, bound).astype(kind)


def setup_inputs(seed: int = 0) -> dict:
    streams_of = jax.random.split(jax.random.key(seed), 8)
    latent = heavy_noise(streams_of[0], (NLAT, NLON, C), 1.0, 6.0, ((0, 16), (1, 16)), (1, 2, 16, 2.0))
    w_first = bell_draw(streams_of[1], (3, 3, C, C), (9 * C) ** -0.5, 0.125)
    w_second = bell_draw(streams_of[2], (3, 3, C, C), (9 * C) ** -0.5, 0.125)
    levels = draw_levels(jax.random.fold_in(streams_of[7], 71), 0)
    prior_scale = jnp.clip(jnp.exp(jax.random.uniform(streams_of[4], (C,), jnp.float32, math.log(0.5), math.log(3.0))), 0.5, 3.0)
    bins = draw_bins(jax.random.fold_in(streams_of[7], 71), 0)
    code_grad = bell_draw(streams_of[6], (NLAT, NLON, C), 1.0, 6.0, ((0, 16), (1, 16)))
    return dict(latent=latent, w_first=w_first, w_second=w_second, levels=levels, prior_scale=prior_scale, bins=bins, code_grad=code_grad)


RATE_WEIGHT = 0.5

def sphere_pad(field):
    half_loop = field.shape[1] // 2
    north_row = jnp.roll(field[0:1], -half_loop, axis=1)
    south_row = jnp.roll(field[-1:], -half_loop, axis=1)
    lat_rows = jnp.concatenate([north_row, field, south_row], axis=0)
    return jnp.concatenate([lat_rows[:, -1:], lat_rows, lat_rows[:, :1]], axis=1)

def pad_adjoint(padded):
    half_loop = (padded.shape[1] - 2) // 2
    lat_rows = padded[:, 1:-1]
    lat_rows = lat_rows.at[:, 0].add(padded[:, -1])
    lat_rows = lat_rows.at[:, -1].add(padded[:, 0])
    interior = lat_rows[1:-1]
    interior = interior.at[0].add(jnp.roll(lat_rows[0], half_loop, axis=0))
    interior = interior.at[-1].add(jnp.roll(lat_rows[-1], half_loop, axis=0))
    return interior

def conv_forward(padded, weight):
    wide = padded.astype(jnp.float32)
    taps = weight.astype(jnp.float32)
    total = jnp.zeros((NLAT, NLON, C), jnp.float32)
    for row_off in range(3):
        for col_off in range(3):
            total = total + jnp.dot(wide[row_off:row_off + NLAT, col_off:col_off + NLON], taps[row_off, col_off], preferred_element_type=jnp.float32)
    return total

def conv_transpose(grad, weight):
    narrow = grad.astype(jnp.float32)
    taps = weight.astype(jnp.float32)
    padded = jnp.zeros((NLAT + 2, NLON + 2, C), jnp.float32)
    for row_off in range(3):
        for col_off in range(3):
            term = jnp.dot(narrow, taps[row_off, col_off].T, preferred_element_type=jnp.float32)
            padded = padded.at[row_off:row_off + NLAT, col_off:col_off + NLON].add(term)
    return pad_adjoint(padded)

def weight_grad(padded, grad):
    wide = padded.astype(jnp.float32)
    narrow = grad.astype(jnp.float32)
    blocks = []
    for row_off in range(3):
        for col_off in range(3):
            window = wide[row_off:row_off + NLAT, col_off:col_off + NLON]
            blocks.append(lax.dot_general(window, narrow, (((0, 1), (0, 1)), ((), ())), preferred_element_type=jnp.float32))
    return jnp.concatenate(blocks, axis=0)

def reference(latent, w_first, w_second, levels, prior_scale, bins, code_grad):
    padded_latent = sphere_pad(latent)
    pre_act = conv_forward(padded_latent, w_first)
    activated = jax.nn.silu(pre_act).astype(jnp.bfloat16)
    padded_act = sphere_pad(activated)
    output = latent.astype(jnp.float32) + conv_forward(padded_act, w_second)
    bounded = jnp.tanh(output)
    half_levels = (levels.astype(jnp.float32) - 1.0) / 2.0
    centred = bins.astype(jnp.float32) - half_levels
    rate_slope = jnp.tanh(centred / (2.0 * prior_scale)) / prior_scale
    grad_out = ((code_grad.astype(jnp.float32) + RATE_WEIGHT * half_levels * rate_slope) * (1.0 - bounded * bounded)).astype(jnp.bfloat16)
    grad_act = conv_transpose(grad_out, w_second)
    sigmoid_pre = jax.nn.sigmoid(pre_act)
    grad_pre = (grad_act * sigmoid_pre * (1.0 + pre_act * (1.0 - sigmoid_pre))).astype(jnp.bfloat16)
    grad_latent = grad_out.astype(jnp.float32) + conv_transpose(grad_pre, w_first)
    cell_scale = 1.0 / math.sqrt(NLAT * NLON)
    grad_first = weight_grad(padded_latent, grad_pre) * cell_scale
    grad_second = weight_grad(padded_act, grad_out) * cell_scale
    return (grad_latent, grad_first, grad_second)
```

```python
import math

import jax
import jax.numpy as jnp
from jax import lax
from jax.experimental import pallas as pl
from jax.experimental.pallas import tpu as pltpu
from jax.sharding import PartitionSpec as P

RATE_WEIGHT = 0.5

F32 = jnp.float32
BF16 = jnp.bfloat16

C = 256
ROWS = 16
COLS = 64
RIM = 4
EXT = ROWS + 2 * RIM
W = 80
N = EXT * W + 16
BASE = 8
TAPS = 2304


def lon_lat():
    return lax.axis_index("lon"), lax.axis_index("lat")


def ring_pairs(step):
    pairs = []
    for lon in range(8):
        circle = [(lon, lat) for lat in range(16)] + [(lon + 8, lat) for lat in reversed(range(16))]
        for i, (lo, la) in enumerate(circle):
            tlo, tla = circle[(i + step) % 32]
            pairs.append((lo * 16 + la, tlo * 16 + tla))
    return pairs


def moved(block, route):
    pairs = []
    for lon in range(16):
        for lat in range(16):
            z, yl, x, yh, core = route(lon // 2, lon % 2, lat // 4, lat // 2 % 2, lat % 2)
            pairs.append((lon * 16 + lat, (z * 2 + yl) * 16 + x * 4 + yh * 2 + core))
    return lax.ppermute(block, ("lon", "lat"), pairs)


def facing(first, second, lon_low, rows, count, mirrored):
    picked = []
    for k in range(count):
        at = rows + jnp.where(mirrored, count - 1 - k, k)
        picked.append(jnp.where(lon_low, first[at].astype(F32), second[at].astype(F32)))
    return picked


def strips_kernel(latent, code, bins, cw, ccw, east, west):
    lon, lat = lon_lat()
    low = lon < 8
    spot = lax.broadcasted_iota(jnp.int32, (EXT * 8, C), 0) % 8

    def gathered(own, start, count, right):
        north = facing(cw, ccw, low, start, count, lat == 0)
        south = facing(ccw, cw, low, start, count, lat == 15)
        cut = slice(56, 64) if right else slice(0, 8)
        wide = own[:, 48:64, :].astype(F32)[:, 8:16] if right else own[:, 0:16, :].astype(F32)[:, 0:8]
        fill = [jnp.zeros((8, C), F32)] * (RIM - count)
        rows = fill + [v[cut] for v in north] + [wide[r] for r in range(ROWS)] + [v[cut] for v in south] + fill
        return jnp.concatenate(rows, axis=0)

    def turned(value, by):
        return pltpu.roll(value, by % (EXT * 8), 0)

    for out, right in ((east, True), (west, False)):
        a = gathered(latent, 0, 4, right)
        b = gathered(code, 4, 2, right)
        c = gathered(bins, 6, 2, right)
        if right:
            a, b = turned(a, -4), turned(b, -2)
        else:
            b, c = turned(b, 4), turned(c, 6)
        out[...] = jnp.where(spot < 4, a, jnp.where(spot < 6, b, c)).astype(BF16)


def put(ref, at, value):
    rows = value.shape[0]
    ref[0, BASE + at : BASE + at + rows, :] = value[:, :128]
    ref[1, BASE + at : BASE + at + rows, :] = value[:, 128:]


def get(ref, at, rows):
    return jnp.concatenate([ref[0, BASE + at : BASE + at + rows, :], ref[1, BASE + at : BASE + at + rows, :]], axis=1)


def spread(dest, ref, start, stop):
    for at in range(start, stop, 320):
        rows = min(320, stop - at)
        for b in range(3):
            for half in range(2):
                lane = b * 256 + half * 128
                dest[at : at + rows, lane : lane + 128] = ref[half, pl.ds(BASE + at + b - 1, rows), :].astype(BF16)


def block_kernel(
    latent, code, bins, cw, ccw, from_east, from_west, w1, w2, w1t, w2t, levels, prior,
    grad_latent, send, keep,
    x32, q32, a32, g32, p32, dact, lat3, act3, go3, gp3, turn,
):
    lon, lat = lon_lat()
    low = lon < 8
    at_north = lat == 0
    at_south = lat == 15
    core = lat % 2

    half_levels = (levels[...].astype(F32) - 1.0) / 2.0
    scale = prior[...]
    double = 2.0 * scale
    weight = RATE_WEIGHT * half_levels

    def cotangent(code_part, bins_part):
        slope = jnp.tanh((bins_part - half_levels) / double) / scale
        return code_part + weight * slope

    north = facing(cw, ccw, low, 0, 4, at_north)
    south = facing(ccw, cw, low, 0, 4, at_south)
    for k in range(4):
        put(x32, k * W + 16, north[k])
        put(x32, (20 + k) * W + 16, south[k])
    for r in range(ROWS):
        put(x32, (4 + r) * W + 16, latent[r].astype(F32))
    north_code = facing(cw, ccw, low, 4, 2, at_north)
    south_code = facing(ccw, cw, low, 4, 2, at_south)
    north_bins = facing(cw, ccw, low, 6, 2, at_north)
    south_bins = facing(ccw, cw, low, 6, 2, at_south)
    for k in range(2):
        put(q32, (2 + k) * W + 16, cotangent(north_code[k], north_bins[k]))
        put(q32, (20 + k) * W + 16, cotangent(south_code[k], south_bins[k]))
    for r in range(ROWS):
        put(q32, (4 + r) * W + 16, cotangent(code[r].astype(F32), bins[r].astype(F32)))

    rows = EXT * 8
    spot = lax.broadcasted_iota(jnp.int32, (rows, C), 0) % 8
    right = from_east[...].astype(F32)
    left = from_west[...].astype(F32)

    def turned(value, by):
        return pltpu.roll(value, by % rows, 0)

    right_x = jnp.where(spot < 4, right, 0.0)
    left_x = jnp.where(spot >= 4, turned(left, 4), 0.0)
    right_q = jnp.where(spot < 2, cotangent(turned(right, -4), turned(right, -6)), 0.0)
    left_q = jnp.where(spot >= 6, cotangent(turned(left, 2), left), 0.0)
    blank = jnp.zeros((8, C), F32)
    put(x32, -8, blank)
    put(x32, 0, blank)
    put(x32, N - 8, blank)
    put(x32, N, blank)
    for r in range(EXT):
        part = slice(r * 8, r * 8 + 8)
        put(x32, (r + 1) * W, right_x[part])
        put(x32, r * W + 8, left_x[part])
        if 2 <= r < 22:
            put(q32, (r + 1) * W, right_q[part])
            put(q32, r * W + 8, left_q[part])
    put(q32, 2 * W, blank)
    put(q32, 22 * W + 8, blank)

    def product(source, at, count, weights, order):
        total = None
        for slot in range(3):
            begin = order[slot]
            if not isinstance(begin, int):
                begin = pl.multiple_of(begin, 256)
            piece = jnp.dot(
                source[at + (slot - 1) * W : at + (slot - 1) * W + count, :],
                weights[pl.ds(begin, 768), :],
                preferred_element_type=F32,
            )
            total = piece if total is None else total + piece
        return total

    plain = (0, 768, 1536)
    top_flip = (jnp.where(at_north, 1536, 0), 768, jnp.where(at_north, 0, 1536))
    low_flip = (jnp.where(at_south, 1536, 0), 768, jnp.where(at_south, 0, 1536))
    above_flip = (jnp.where(at_north, 1536, 0), 768, 1536)
    below_flip = (0, 768, jnp.where(at_south, 0, 1536))

    def pieces(first, last, top, bottom, orders):
        cuts = [(first, top, orders[0])]
        middle = (bottom - top) // 2
        cuts += [(top, top + middle, plain), (top + middle, bottom, plain)]
        cuts += [(bottom, last, orders[1])]
        out = []
        for i, (start, stop, order) in enumerate(cuts):
            out.append((start * W, (stop - start) * W + 16, 8 if i else 0, order))
        return out

    spread(lat3, x32, 0, N)
    for at, count, skip, order in pieces(1, 23, 4, 20, (top_flip, low_flip)):
        pre = product(lat3, at, count, w1, order)[skip:]
        sig = jax.nn.sigmoid(pre)
        put(dact, at + skip, sig * (1.0 + pre * (1.0 - sig)))
        put(a32, at + skip, pre * sig)

    spread(act3, a32, W, 23 * W + 16)
    for at, count, skip, order in pieces(2, 22, 4, 20, (top_flip, low_flip)):
        conv = product(act3, at, count, w2, order)[skip:]
        size = count - skip
        bounded = jnp.tanh(get(x32, at + skip, size) + conv)
        out = get(q32, at + skip, size) * (1.0 - bounded * bounded)
        put(g32, at + skip, out.astype(BF16).astype(F32))

    def own_cells(source, shift):
        return jnp.concatenate(
            [source[(r + shift) * W + 16 : (r + shift) * W + 80, :] for r in range(4, 20)], axis=0
        )

    def weight_grad(source, grad3, lane):
        turn[...] = jnp.transpose(own_cells(grad3.at[:, 256:512], 0))
        for a in range(3):
            full = jnp.dot(turn[...], own_cells(source, a - 1), preferred_element_type=F32)
            full = full.reshape(8, 2, 16, 768) * (1.0 / 512.0)
            mine = jnp.where(core == 0, full[:, 0], full[:, 1])
            other = jnp.where(core == 0, full[:, 1], full[:, 0])
            keep[:, :, lane + 768 * a : lane + 768 * (a + 1)] = mine
            send[:, :, lane + 768 * a : lane + 768 * (a + 1)] = other.astype(BF16)

    spread(go3, g32, 2 * W, 22 * W + 16)
    weight_grad(act3, go3, TAPS)

    for at, count, skip, order in pieces(3, 21, 5, 19, (above_flip, below_flip)):
        back = product(go3, at, count, w2t, order)[skip:]
        grad = back * get(dact, at + skip, count - skip)
        put(p32, at + skip, grad)

    spread(gp3, p32, 3 * W, 21 * W + 16)
    weight_grad(lat3, gp3, 0)

    def rows_of(first, count):
        return jnp.concatenate([gp3[r * W + 16 : r * W + 80, :] for r in range(first, first + count)], axis=0)

    def tapped(first, count, begin):
        if not isinstance(begin, int):
            begin = pl.multiple_of(begin, 256)
        return jnp.dot(rows_of(first, count), w1t[pl.ds(begin, 768), :], preferred_element_type=F32)

    above = jnp.concatenate([tapped(3, 1, above_flip[0]), tapped(4, 15, 0)], axis=0)
    below = jnp.concatenate([tapped(5, 15, 1536), tapped(20, 1, below_flip[2])], axis=0)
    total = tapped(4, 16, 768) + above + below
    for r in range(ROWS):
        grad_latent[r] = total[r * COLS : (r + 1) * COLS] + get(g32, (4 + r) * W + 16, COLS)


def after_core_kernel(keep, got, own, s1, s2, s3):
    lon, lat = lon_lat()
    x = lat // 4

    def part(to):
        return keep[pl.ds(2 * to, 2)] + got[pl.ds(2 * to, 2)].astype(F32)

    own[...] = part(x)
    for k, out in ((1, s1), (2, s2), (3, s3)):
        out[...] = part((x + k) % 4).astype(BF16)


def after_x_kernel(own_in, r1, r2, r3, own, s1, s2, s3, parts):
    lon, lat = lon_lat()
    yl, yh = lon % 2, lat // 2 % 2
    for h in range(2):
        total = own_in[h] + r1[h].astype(F32) + r2[h].astype(F32) + r3[h].astype(F32)
        for tensor in range(2):
            for j in range(16):
                lane = tensor * TAPS + 144 * j
                parts[j % 2, h, j // 2, 16 * tensor : 16 * tensor + 16, :] = total[:, lane : lane + 144]
    own[...] = parts[yl, yh]
    s1[...] = parts[1 - yl, yh].astype(BF16)
    s2[...] = parts[yl, 1 - yh].astype(BF16)
    s3[...] = parts[1 - yl, 1 - yh].astype(BF16)


def after_y_kernel(own_in, r1, r2, r3, own, s1):
    lon, lat = lon_lat()
    odd = lon // 2 % 2
    for k in range(4):
        even_part = own_in[2 * k] + r1[2 * k].astype(F32) + r2[2 * k].astype(F32) + r3[2 * k].astype(F32)
        odd_part = own_in[2 * k + 1] + r1[2 * k + 1].astype(F32) + r2[2 * k + 1].astype(F32) + r3[2 * k + 1].astype(F32)
        own[k] = jnp.where(odd == 0, even_part, odd_part)
        s1[k] = jnp.where(odd == 0, odd_part, even_part)


def after_pair_kernel(own_in, r1, own, s1, s2, s3):
    lon, lat = lon_lat()
    far = lon // 4
    own[...] = own_in[far] + r1[far]
    for k, out in ((1, s1), (2, s2), (3, s3)):
        to = (far + k) % 4
        out[...] = own_in[to] + r1[to]


def last_kernel(own_in, r1, r2, r3, first, second):
    total = own_in[...] + r1[...] + r2[...] + r3[...]
    first[...] = jnp.transpose(total[0:16])
    second[...] = jnp.transpose(total[16:32])


def local_call(kernel, outs, scratch=()):
    whole = pl.BlockSpec(memory_space=pltpu.VMEM)

    def call(*operands):
        return pl.pallas_call(
            kernel,
            out_shape=[jax.ShapeDtypeStruct(shape, kind) for shape, kind in outs],
            in_specs=[whole] * len(operands),
            out_specs=[whole] * len(outs),
            scratch_shapes=list(scratch),
            compiler_params=pltpu.CompilerParams(vmem_limit_bytes=60 * 1024 * 1024),
        )(*operands)

    return call


def summed(send, keep):
    got = moved(send, lambda z, yl, x, yh, core: (z, yl, x, yh, 1 - core))
    size = (2, 16, 2 * TAPS)
    own, s1, s2, s3 = local_call(after_core_kernel, [(size, F32)] + [(size, BF16)] * 3)(keep, got)
    r1, r2, r3 = [
        moved(s, lambda z, yl, x, yh, core, k=k: (z, yl, (x + k) % 4, yh, core)) for k, s in ((1, s1), (2, s2), (3, s3))
    ]
    size = (8, 32, 144)
    own, s1, s2, s3 = local_call(
        after_x_kernel, [(size, F32)] + [(size, BF16)] * 3, [pltpu.VMEM((2, 2) + size, F32)]
    )(own, r1, r2, r3)
    r1 = moved(s1, lambda z, yl, x, yh, core: (z, 1 - yl, x, yh, core))
    r2 = moved(s2, lambda z, yl, x, yh, core: (z, yl, x, 1 - yh, core))
    r3 = moved(s3, lambda z, yl, x, yh, core: (z, 1 - yl, x, 1 - yh, core))
    size = (4, 32, 144)
    own, s1 = local_call(after_y_kernel, [(size, F32)] * 2)(own, r1, r2, r3)
    r1 = moved(s1, lambda z, yl, x, yh, core: (z ^ 1, yl, x, yh, core))
    size = (32, 144)
    own, s1, s2, s3 = local_call(after_pair_kernel, [(size, F32)] * 4)(own, r1)
    r1, r2, r3 = [
        moved(s, lambda z, yl, x, yh, core, k=k: ((z + 2 * k) % 8, yl, x, yh, core)) for k, s in ((1, s1), (2, s2), (3, s3))
    ]
    return local_call(last_kernel, [((144, 16), F32)] * 2)(own, r1, r2, r3)


def turned_weight(weight):
    return weight[::-1, ::-1].transpose(0, 1, 3, 2).reshape(TAPS, C)


def on_device(latent, w_first, w_second, levels, prior_scale, bins, code_grad):
    lon, lat = lon_lat()
    low = lon < 8

    def edge(last):
        start = jnp.where(last, ROWS, 0)
        four = lax.dynamic_slice_in_dim(latent, jnp.where(last, ROWS - 4, 0), 4, 0)
        code = lax.dynamic_slice_in_dim(code_grad, jnp.where(last, ROWS - 2, 0), 2, 0)
        bin_rows = lax.dynamic_slice_in_dim(bins, jnp.where(last, ROWS - 2, 0), 2, 0).astype(BF16)
        return jnp.concatenate([four, code, bin_rows], axis=0)

    cw = lax.ppermute(edge(low), ("lon", "lat"), ring_pairs(1))
    ccw = lax.ppermute(edge(jnp.logical_not(low)), ("lon", "lat"), ring_pairs(-1))
    strip = ((EXT * 8, C), BF16)
    east, west = local_call(strips_kernel, [strip] * 2)(latent, code_grad, bins, cw, ccw)
    count = lax.axis_size("lon")
    from_west = lax.ppermute(east, "lon", [(i, (i + 1) % count) for i in range(count)])
    from_east = lax.ppermute(west, "lon", [((i + 1) % count, i) for i in range(count)])

    frame = pltpu.VMEM((2, N + 2 * BASE, 128), F32)
    triple = pltpu.VMEM((N, 3 * C), BF16)
    grad_latent, send, keep = local_call(
        block_kernel,
        [((ROWS, COLS, C), F32), ((8, 16, 2 * TAPS), BF16), ((8, 16, 2 * TAPS), F32)],
        [frame] * 6 + [triple] * 4 + [pltpu.VMEM((C, ROWS * COLS), BF16)],
    )(
        latent, code_grad, bins, cw, ccw, from_east, from_west,
        w_first.reshape(TAPS, C), w_second.reshape(TAPS, C), turned_weight(w_first), turned_weight(w_second),
        levels.reshape(1, C), prior_scale.reshape(1, C),
    )
    grad_first, grad_second = summed(send, keep)
    return (grad_latent, grad_first, grad_second)


def solution(mesh):
    placed = (
        P("lat", "lon", None),
        P(),
        P(),
        P(),
        P(),
        P("lat", "lon", None),
        P("lat", "lon", None),
    )
    return jax.shard_map(
        on_device,
        mesh=mesh,
        in_specs=placed,
        out_specs=(P("lat", "lon", None), P("lon", "lat"), P("lon", "lat")),
        check_vma=False,
    )
```

```python
import jax
import jax.numpy as jnp
from jax import lax
from jax.experimental import pallas as pl
from jax.experimental.pallas import tpu as pltpu
from jax.sharding import Mesh
from jax.sharding import PartitionSpec as P

RATE_WEIGHT = 0.5

F32 = jnp.float32
BF16 = jnp.bfloat16

C = 256
ROWS = 16
COLS = 64
RIM = 4
EXT = ROWS + 2 * RIM
W = 80
N = EXT * W + 16
BASE = 8
TAPS = 2304


def place():
    lon = 2 * lax.axis_index("z") + lax.axis_index("yl")
    lat = 4 * lax.axis_index("x") + 2 * lax.axis_index("yh") + lax.axis_index("core")
    return lon, lat


FINE = ("z", "yl", "x", "yh", "core")


def ring_pairs(step):
    pairs = []
    for lon in range(8):
        circle = [(lon, lat) for lat in range(16)] + [(lon + 8, lat) for lat in reversed(range(16))]
        for i, (lo, la) in enumerate(circle):
            tlo, tla = circle[(i + step) % 32]
            pairs.append((lo * 16 + la, tlo * 16 + tla))
    return pairs


def slanted_pairs(step, side):
    return [(a, (b // 16 + side) % 16 * 16 + b % 16) for a, b in ring_pairs(step)]


def moved(block, route):
    pairs = []
    for lon in range(16):
        for lat in range(16):
            z, yl, x, yh, core = route(lon // 2, lon % 2, lat // 4, lat // 2 % 2, lat % 2)
            pairs.append((lon * 16 + lat, (z * 2 + yl) * 16 + x * 4 + yh * 2 + core))
    return lax.ppermute(block, FINE, pairs)


def cotangent_of(levels, prior):
    half_levels = (levels[...].astype(F32) - 1.0) / 2.0
    scale = prior[...]
    double = 2.0 * scale
    weight = RATE_WEIGHT * half_levels

    def cotangent(code_part, bins_part):
        slope = jnp.tanh((bins_part - half_levels) / double) / scale
        return code_part + weight * slope

    return cotangent


def fetched(pairs, arrived):
    copies = [pltpu.make_async_copy(far, near, arrived.at[i]) for i, (far, near) in enumerate(pairs)]
    for copy in copies:
        copy.start()
    return copies


def rims_kernel(
    latent_far, code_far, bins_far, levels_far, prior_far,
    cw, ccw, east, west, cw_east, cw_west, ccw_east, ccw_west,
    latent, code, bins, levels, prior, arrived,
):
    pairs = (
        (latent_far, latent), (code_far, code), (bins_far, bins), (levels_far, levels), (prior_far, prior),
    )
    for copy in fetched(pairs, arrived):
        copy.wait()
    lon, lat = place()
    low = lon < 8
    cotangent = cotangent_of(levels, prior)

    def outward(k, first, last):
        cw[k] = jnp.where(low, last, first).astype(BF16)
        ccw[k] = jnp.where(low, first, last).astype(BF16)

    for k in range(4):
        outward(k, latent[k].astype(F32), latent[12 + k].astype(F32))
    for k in range(2):
        outward(
            4 + k,
            cotangent(code[k].astype(F32), bins[k].astype(F32)),
            cotangent(code[14 + k].astype(F32), bins[14 + k].astype(F32)),
        )

    spot = lax.broadcasted_iota(jnp.int32, (ROWS * 8, C), 0) % 8
    for out, cw_out, ccw_out, right in ((east, cw_east, ccw_east, True), (west, cw_west, ccw_west, False)):
        tile = slice(48, 64) if right else slice(0, 16)
        side = slice(8, 16) if right else slice(0, 8)
        x = latent[:, tile, :].astype(F32)[:, side].reshape(ROWS * 8, C)
        q = cotangent(
            code[:, tile, :].astype(F32)[:, side].reshape(ROWS * 8, C),
            bins[:, tile, :].astype(F32)[:, side].reshape(ROWS * 8, C),
        )
        if right:
            x = pltpu.roll(x, ROWS * 8 - 4, 0)
            q = pltpu.roll(q, ROWS * 8 - 2, 0)
        else:
            q = pltpu.roll(q, 4, 0)
        both = jnp.where(spot < 4, x, q)
        out[...] = both.astype(BF16)
        first, last = both[:32], both[96:]
        cw_out[...] = jnp.where(low, last, first).astype(BF16)
        ccw_out[...] = jnp.where(low, first, last).astype(BF16)


def facing(first, second, low, rows, count, mirrored):
    picked = []
    for k in range(count):
        at = rows + jnp.where(mirrored, count - 1 - k, k)
        picked.append(jnp.where(low, first[at].astype(F32), second[at].astype(F32)))
    return picked


def put(ref, at, value):
    rows = value.shape[0]
    ref[0, BASE + at : BASE + at + rows, :] = value[:, :128]
    ref[1, BASE + at : BASE + at + rows, :] = value[:, 128:]


def get(ref, at, rows):
    return jnp.concatenate([ref[0, BASE + at : BASE + at + rows, :], ref[1, BASE + at : BASE + at + rows, :]], axis=1)


def spread(dest, ref, start, stop):
    for at in range(start, stop, 320):
        rows = min(320, stop - at)
        for b in range(3):
            for half in range(2):
                lane = b * 256 + half * 128
                dest[at : at + rows, lane : lane + 128] = ref[half, pl.ds(BASE + at + b - 1, rows), :].astype(BF16)


def block_kernel(*refs):
    fars = refs[:15]
    grad_latent, send, keep = refs[15:18]
    nears = refs[18:33]
    x32, q32, a32, g32, dact, lat3, act3, go3, gp3, turn, arrived = refs[33:]
    fetches = fetched(tuple(zip(fars, nears)), arrived)
    latent, code, bins, w1, cw, ccw, from_east, from_west, cw_east, cw_west, ccw_east, ccw_west, levels, prior, w2 = nears
    p32 = a32
    for fetch in fetches[:3] + fetches[4:14]:
        fetch.wait()
    lon, lat = place()
    low = lon < 8
    at_north = lat == 0
    at_south = lat == 15
    core = lat % 2
    cotangent = cotangent_of(levels, prior)

    north = facing(cw, ccw, low, 0, 4, at_north)
    south = facing(ccw, cw, low, 0, 4, at_south)
    for k in range(4):
        put(x32, k * W + 16, north[k])
        put(x32, (20 + k) * W + 16, south[k])
    for r in range(ROWS):
        put(x32, (4 + r) * W + 16, latent[r].astype(F32))
    north_q = facing(cw, ccw, low, 4, 2, at_north)
    south_q = facing(ccw, cw, low, 4, 2, at_south)
    for k in range(2):
        put(q32, (2 + k) * W + 16, north_q[k])
        put(q32, (20 + k) * W + 16, south_q[k])
    for r in range(ROWS):
        put(q32, (4 + r) * W + 16, cotangent(code[r].astype(F32), bins[r].astype(F32)))

    rows = EXT * 8
    spot = lax.broadcasted_iota(jnp.int32, (rows, C), 0) % 8

    def column(own, cw_part, ccw_part, beside):
        side_low = beside < 8
        one, two = cw_part[...].astype(F32), ccw_part[...].astype(F32)

        def end(value, mirrored):
            tiles = [value[8 * k : 8 * k + 8] for k in range(4)]
            return jnp.where(mirrored, jnp.concatenate(tiles[::-1], axis=0), value)

        north = end(jnp.where(side_low, one, two), at_north)
        south = end(jnp.where(side_low, two, one), at_south)
        return jnp.concatenate([north, own[...].astype(F32), south], axis=0)

    left = column(from_west, cw_east, ccw_east, (lon + 15) % 16)
    right = column(from_east, cw_west, ccw_west, (lon + 1) % 16)

    def turned(value, by):
        return pltpu.roll(value, by % rows, 0)

    right_x = jnp.where(spot < 4, right, 0.0)
    left_x = jnp.where(spot >= 4, turned(left, 4), 0.0)
    right_q = jnp.where(spot < 2, turned(right, -4), 0.0)
    left_q = jnp.where(spot >= 6, turned(left, 2), 0.0)
    blank = jnp.zeros((8, C), F32)
    put(x32, -8, blank)
    put(x32, 0, blank)
    put(x32, N - 8, blank)
    put(x32, N, blank)
    for r in range(EXT):
        part = slice(r * 8, r * 8 + 8)
        put(x32, (r + 1) * W, right_x[part])
        put(x32, r * W + 8, left_x[part])
        if 2 <= r < 22:
            put(q32, (r + 1) * W, right_q[part])
            put(q32, r * W + 8, left_q[part])
    put(q32, 2 * W, blank)
    put(q32, 22 * W + 8, blank)

    def product(source, at, count, weights, order):
        total = None
        for slot in range(3):
            begin = order[slot]
            if not isinstance(begin, int):
                begin = pl.multiple_of(begin, 256)
            piece = jnp.dot(
                source[at + (slot - 1) * W : at + (slot - 1) * W + count, :],
                weights[pl.ds(begin, 768), :],
                preferred_element_type=F32,
            )
            total = piece if total is None else total + piece
        return total

    def returned(parts, weights, a):
        total = None
        for b in range(3):
            begin = (3 * a + 2 - b) * 256
            if not isinstance(begin, int):
                begin = pl.multiple_of(begin, 256)
            piece = lax.dot_general(
                parts[:, 256 * b : 256 * (b + 1)],
                weights[pl.ds(begin, 256), :],
                (((1,), (1,)), ((), ())),
                preferred_element_type=F32,
            )
            total = piece if total is None else total + piece
        return total

    plain = (0, 768, 1536)
    top_flip = (jnp.where(at_north, 1536, 0), 768, jnp.where(at_north, 0, 1536))
    low_flip = (jnp.where(at_south, 1536, 0), 768, jnp.where(at_south, 0, 1536))
    above_tap = jnp.where(at_north, 0, 2)
    below_tap = jnp.where(at_south, 2, 0)

    def pieces(first, last, top, bottom, orders, plain=plain):
        cuts = [(first, top, orders[0])]
        middle = (bottom - top) // 2
        cuts += [(top, top + middle, plain), (top + middle, bottom, plain)]
        cuts += [(bottom, last, orders[1])]
        out = []
        for i, (start, stop, order) in enumerate(cuts):
            out.append((start * W, (stop - start) * W + 16, 8 if i else 0, order))
        return out

    spread(lat3, x32, 0, N)
    fetches[3].wait()
    for at, count, skip, order in pieces(1, 23, 4, 20, (top_flip, low_flip)):
        pre = product(lat3, at, count, w1, order)[skip:]
        sig = jax.nn.sigmoid(pre)
        put(dact, at + skip, sig * (1.0 + pre * (1.0 - sig)))
        put(a32, at + skip, pre * sig)

    spread(act3, a32, W, 23 * W + 16)
    fetches[14].wait()
    for at, count, skip, order in pieces(2, 22, 4, 20, (top_flip, low_flip)):
        conv = product(act3, at, count, w2, order)[skip:]
        size = count - skip
        bounded = jnp.tanh(get(x32, at + skip, size) + conv)
        out = get(q32, at + skip, size) * (1.0 - bounded * bounded)
        put(g32, at + skip, out.astype(BF16).astype(F32))

    def own_cells(source, shift):
        return jnp.concatenate(
            [source[(r + shift) * W + 16 : (r + shift) * W + 80, :] for r in range(4, 20)], axis=0
        )

    def weight_grad(source, grad3, lane):
        turn[...] = jnp.transpose(own_cells(grad3.at[:, 256:512], 0))
        for a in range(3):
            full = jnp.dot(turn[...], own_cells(source, a - 1), preferred_element_type=F32)
            full = full.reshape(8, 2, 16, 768) * (1.0 / 512.0)
            mine = jnp.where(core == 0, full[:, 0], full[:, 1])
            other = jnp.where(core == 0, full[:, 1], full[:, 0])
            keep[:, :, lane + 768 * a : lane + 768 * (a + 1)] = mine
            send[:, :, lane + 768 * a : lane + 768 * (a + 1)] = other.astype(BF16)

    spread(go3, g32, 2 * W, 22 * W + 16)
    weight_grad(act3, go3, TAPS)

    taps = ((above_tap, 1, 0), (2, 1, below_tap))
    for at, count, skip, order in pieces(3, 21, 5, 19, taps, (2, 1, 0)):
        back = None
        for slot in range(3):
            begin = at + (slot - 1) * W
            piece = returned(go3[begin : begin + count, :], w2, order[slot])
            back = piece if back is None else back + piece
        back = back[skip:]
        grad = back * get(dact, at + skip, count - skip)
        put(p32, at + skip, grad)

    spread(gp3, p32, 3 * W, 21 * W + 16)
    weight_grad(lat3, gp3, 0)

    def rows_of(first, count):
        return jnp.concatenate([gp3[r * W + 16 : r * W + 80, :] for r in range(first, first + count)], axis=0)

    def tapped(first, count, a):
        return returned(rows_of(first, count), w1, a)

    above = jnp.concatenate([tapped(3, 1, above_tap), tapped(4, 15, 2)], axis=0)
    below = jnp.concatenate([tapped(5, 15, 0), tapped(20, 1, below_tap)], axis=0)
    total = tapped(4, 16, 1) + above + below
    for r in range(ROWS):
        grad_latent[r] = total[r * COLS : (r + 1) * COLS] + get(g32, (4 + r) * W + 16, COLS)


def after_core_kernel(keep, got, own, s1, s2, s3):
    x = lax.axis_index("x")

    def part(to):
        return keep[pl.ds(2 * to, 2)] + got[pl.ds(2 * to, 2)].astype(F32)

    own[...] = part(x)
    for k, out in ((1, s1), (2, s2), (3, s3)):
        out[...] = part((x + k) % 4).astype(BF16)


def after_x_kernel(own_in, r1, r2, r3, own, s1, s2, s3, parts):
    yl, yh = lax.axis_index("yl"), lax.axis_index("yh")
    for h in range(2):
        total = own_in[h] + r1[h].astype(F32) + r2[h].astype(F32) + r3[h].astype(F32)
        for tensor in range(2):
            for odd in range(2):
                lanes = [tensor * TAPS + 144 * (2 * z + odd) for z in range(8)]
                chosen = jnp.concatenate([total[:, lane : lane + 144] for lane in lanes], axis=1)
                parts[odd, h, 16 * tensor : 16 * tensor + 16, :] = chosen
    own[...] = parts[yl, yh]
    s1[...] = parts[1 - yl, yh].astype(BF16)
    s2[...] = parts[yl, 1 - yh].astype(BF16)
    s3[...] = parts[1 - yl, 1 - yh].astype(BF16)


def after_y_kernel(own_in, r1, r2, r3, out):
    total = own_in[...] + r1[...].astype(F32) + r2[...].astype(F32) + r3[...].astype(F32)
    for z in range(8):
        out[z] = total[:, 144 * z : 144 * z + 144].astype(BF16)


def local_call(kernel, outs, scratch=(), near=True, room=8, far_ins=(), near_outs=None):
    whole = pl.BlockSpec(memory_space=pltpu.VMEM)
    far = pl.BlockSpec(memory_space=pl.ANY)

    def call(*operands):
        if near:
            operands = [pltpu.with_memory_space_constraint(v, pltpu.VMEM) for v in operands]
        shapes = [
            pltpu.VMEM(shape, kind) if near_outs is None or i in near_outs else jax.ShapeDtypeStruct(shape, kind)
            for i, (shape, kind) in enumerate(outs)
        ]
        return pl.pallas_call(
            kernel,
            out_shape=shapes,
            in_specs=[far if i in far_ins else whole for i in range(len(operands))],
            out_specs=[whole] * len(outs),
            scratch_shapes=list(scratch),
            compiler_params=pltpu.CompilerParams(vmem_limit_bytes=room * 1024 * 1024),
        )(*operands)

    return call


def summed(send, keep):
    got = lax.ppermute(send, "core", [(0, 1), (1, 0)])
    size = (2, 16, 2 * TAPS)
    own, s1, s2, s3 = local_call(after_core_kernel, [(size, F32)] + [(size, BF16)] * 3)(keep, got)
    r1, r2, r3 = [
        moved(s, lambda z, yl, x, yh, core, k=k: (z, yl, (x + k) % 4, yh, core)) for k, s in ((1, s1), (2, s2), (3, s3))
    ]
    size = (32, TAPS // 2)
    own, s1, s2, s3 = local_call(
        after_x_kernel, [(size, F32)] + [(size, BF16)] * 3, [pltpu.VMEM((2, 2) + size, F32)]
    )(own, r1, r2, r3)
    r1 = moved(s1, lambda z, yl, x, yh, core: (z, 1 - yl, x, yh, core))
    r2 = moved(s2, lambda z, yl, x, yh, core: (z, yl, x, 1 - yh, core))
    r3 = moved(s3, lambda z, yl, x, yh, core: (z, 1 - yl, x, 1 - yh, core))
    (parts,) = local_call(after_y_kernel, [((8, 32, 144), BF16)])(own, r1, r2, r3)
    parts = lax.all_to_all(parts, "z", 0, 0)
    total = jnp.sum(parts.astype(F32), axis=0)
    return total[:16].T, total[16:].T


def on_device(latent, w_first, w_second, levels, prior_scale, bins, code_grad):
    levels = levels.reshape(1, C)
    prior = prior_scale.reshape(1, C)
    given = [pltpu.with_memory_space_constraint(v, pltpu.HBM) for v in (latent, code_grad, bins, levels, prior)]
    edge = ((6, COLS, C), BF16)
    strip = ((ROWS * 8, C), BF16)
    corner = ((32, C), BF16)
    cells = (ROWS, COLS, C)
    cw, ccw, east, west, cw_east, cw_west, ccw_east, ccw_west = local_call(
        rims_kernel,
        [edge, edge, strip, strip] + [corner] * 4,
        [pltpu.VMEM(v.shape, v.dtype) for v in given] + [pltpu.SemaphoreType.DMA((5,))],
        near=False, far_ins=range(5),
    )(*given)
    cw = lax.ppermute(cw, FINE, ring_pairs(1))
    ccw = lax.ppermute(ccw, FINE, ring_pairs(-1))
    from_west = lax.ppermute(east, ("z", "yl"), [(i, (i + 1) % 16) for i in range(16)])
    from_east = lax.ppermute(west, ("z", "yl"), [((i + 1) % 16, i) for i in range(16)])
    cw_east = lax.ppermute(cw_east, FINE, slanted_pairs(1, 1))
    cw_west = lax.ppermute(cw_west, FINE, slanted_pairs(1, -1))
    ccw_east = lax.ppermute(ccw_east, FINE, slanted_pairs(-1, 1))
    ccw_west = lax.ppermute(ccw_west, FINE, slanted_pairs(-1, -1))

    frame = pltpu.VMEM((2, N + 2 * BASE, 128), F32)
    triple = pltpu.VMEM((N, 3 * C), BF16)
    w1, w2 = [pltpu.with_memory_space_constraint(w.reshape(TAPS, C), pltpu.HBM) for w in (w_first, w_second)]
    fars = given[:3] + [w1, cw, ccw, from_east, from_west, cw_east, cw_west, ccw_east, ccw_west] + given[3:] + [w2]
    grad_latent, send, keep = local_call(
        block_kernel,
        [(cells, F32), ((8, 16, 2 * TAPS), BF16), ((8, 16, 2 * TAPS), F32)],
        [pltpu.VMEM(v.shape, v.dtype) for v in fars]
        + [frame] * 5 + [triple] * 4 + [pltpu.VMEM((C, ROWS * COLS), BF16), pltpu.SemaphoreType.DMA((15,))],
        near=False, room=44, far_ins=range(15), near_outs=(1, 2),
    )(*fars)
    grad_first, grad_second = summed(send, keep)
    return (grad_latent, grad_first, grad_second)


def solution(mesh):
    fine = Mesh(mesh.devices.reshape(8, 2, 4, 2, 2), FINE)
    lon, lat = ("z", "yl"), ("x", "yh", "core")
    placed = (P(lat, lon, None), P(), P(), P(), P(), P(lat, lon, None), P(lat, lon, None))
    return jax.shard_map(
        on_device,
        mesh=fine,
        in_specs=placed,
        out_specs=(P(lat, lon, None), P(lon, lat), P(lon, lat)),
        check_vma=False,
    )
```

```python
import jax
import jax.numpy as jnp
from jax import lax
from jax.experimental import pallas as pl
from jax.experimental.pallas import tpu as pltpu
from jax.sharding import Mesh
from jax.sharding import PartitionSpec as P

RATE_WEIGHT = 0.5

F32 = jnp.float32
BF16 = jnp.bfloat16

C = 256
ROWS = 16
COLS = 64
RIM = 4
EXT = ROWS + 2 * RIM
W = 80
N = EXT * W + 16
BASE = 8
TAPS = 2304


def place():
    lon = 2 * lax.axis_index("z") + lax.axis_index("yl")
    lat = 4 * lax.axis_index("x") + 2 * lax.axis_index("yh") + lax.axis_index("core")
    return lon, lat


FINE = ("z", "yl", "x", "yh", "core")


def ring_pairs(step):
    pairs = []
    for lon in range(8):
        circle = [(lon, lat) for lat in range(16)] + [(lon + 8, lat) for lat in reversed(range(16))]
        for i, (lo, la) in enumerate(circle):
            tlo, tla = circle[(i + step) % 32]
            pairs.append((lo * 16 + la, tlo * 16 + tla))
    return pairs


def moved(block, route):
    pairs = []
    for lon in range(16):
        for lat in range(16):
            z, yl, x, yh, core = route(lon // 2, lon % 2, lat // 4, lat // 2 % 2, lat % 2)
            pairs.append((lon * 16 + lat, (z * 2 + yl) * 16 + x * 4 + yh * 2 + core))
    return lax.ppermute(block, FINE, pairs)


def cotangent_of(levels, prior):
    half_levels = (levels[...].astype(F32) - 1.0) / 2.0
    scale = prior[...]
    double = 2.0 * scale
    weight = RATE_WEIGHT * half_levels

    def cotangent(code_part, bins_part):
        slope = jnp.tanh((bins_part - half_levels) / double) / scale
        return code_part + weight * slope

    return cotangent


def fetched(pairs, arrived):
    copies = [pltpu.make_async_copy(far, near, arrived.at[i]) for i, (far, near) in enumerate(pairs)]
    for copy in copies:
        copy.start()
    return copies


def rims_kernel(
    latent_far, code_far, bins_far, levels_far, prior_far,
    cw, ccw, east, west,
    latent, code, bins, levels, prior, arrived,
):
    pairs = (
        (latent_far, latent), (code_far, code), (bins_far, bins), (levels_far, levels), (prior_far, prior),
    )
    for copy in fetched(pairs, arrived):
        copy.wait()
    lon, lat = place()
    low = lon < 8
    cotangent = cotangent_of(levels, prior)

    def outward(k, first, last):
        cw[k] = jnp.where(low, last, first).astype(BF16)
        ccw[k] = jnp.where(low, first, last).astype(BF16)

    for k in range(4):
        outward(k, latent[k].astype(F32), latent[12 + k].astype(F32))
    for k in range(2):
        outward(
            4 + k,
            cotangent(code[k].astype(F32), bins[k].astype(F32)),
            cotangent(code[14 + k].astype(F32), bins[14 + k].astype(F32)),
        )

    spot = lax.broadcasted_iota(jnp.int32, (ROWS * 8, C), 0) % 8
    for out, right in ((east, True), (west, False)):
        tile = slice(48, 64) if right else slice(0, 16)
        side = slice(8, 16) if right else slice(0, 8)
        x = latent[:, tile, :].astype(F32)[:, side].reshape(ROWS * 8, C)
        q = cotangent(
            code[:, tile, :].astype(F32)[:, side].reshape(ROWS * 8, C),
            bins[:, tile, :].astype(F32)[:, side].reshape(ROWS * 8, C),
        )
        if right:
            x = pltpu.roll(x, ROWS * 8 - 4, 0)
            q = pltpu.roll(q, ROWS * 8 - 2, 0)
        else:
            q = pltpu.roll(q, 4, 0)
        out[...] = jnp.where(spot < 4, x, q).astype(BF16)


def corners_kernel(from_west, from_east, cw_corner, ccw_corner):
    lon, lat = place()
    low = lon < 8
    for side, strip in enumerate((from_west, from_east)):
        first, last = strip[0:32, :].astype(F32), strip[96:128, :].astype(F32)
        cw_corner[32 * side : 32 * side + 32, :] = jnp.where(low, last, first).astype(BF16)
        ccw_corner[32 * side : 32 * side + 32, :] = jnp.where(low, first, last).astype(BF16)


def facing(first, second, low, rows, count, mirrored):
    picked = []
    for k in range(count):
        at = rows + jnp.where(mirrored, count - 1 - k, k)
        picked.append(jnp.where(low, first[at].astype(F32), second[at].astype(F32)))
    return picked


def put(ref, at, value):
    rows = value.shape[0]
    ref[0, BASE + at : BASE + at + rows, :] = value[:, :128]
    ref[1, BASE + at : BASE + at + rows, :] = value[:, 128:]


def get(ref, at, rows):
    return jnp.concatenate([ref[0, BASE + at : BASE + at + rows, :], ref[1, BASE + at : BASE + at + rows, :]], axis=1)


def spread(dest, ref, start, stop):
    for at in range(start, stop, 320):
        rows = min(320, stop - at)
        for b in range(3):
            for half in range(2):
                lane = b * 256 + half * 128
                dest[at : at + rows, lane : lane + 128] = ref[half, pl.ds(BASE + at + b - 1, rows), :].astype(BF16)


def block_kernel(*refs):
    fars = refs[:13]
    grad_latent, send, keep = refs[13:16]
    nears = refs[16:29]
    x32, q32, a32, g32, dact, lat3, act3, go3, gp3, turn, arrived = refs[29:]
    fetches = fetched(tuple(zip(fars, nears)), arrived)
    latent, code, bins, w1, cw, ccw, from_east, from_west, cw_corner, ccw_corner, levels, prior, w2 = nears
    p32 = a32
    for fetch in fetches[:3] + fetches[4:12]:
        fetch.wait()
    lon, lat = place()
    low = lon < 8
    at_north = lat == 0
    at_south = lat == 15
    core = lat % 2
    cotangent = cotangent_of(levels, prior)

    north = facing(cw, ccw, low, 0, 4, at_north)
    south = facing(ccw, cw, low, 0, 4, at_south)
    for k in range(4):
        put(x32, k * W + 16, north[k])
        put(x32, (20 + k) * W + 16, south[k])
    for r in range(ROWS):
        put(x32, (4 + r) * W + 16, latent[r].astype(F32))
    north_q = facing(cw, ccw, low, 4, 2, at_north)
    south_q = facing(ccw, cw, low, 4, 2, at_south)
    for k in range(2):
        put(q32, (2 + k) * W + 16, north_q[k])
        put(q32, (20 + k) * W + 16, south_q[k])
    for r in range(ROWS):
        put(q32, (4 + r) * W + 16, cotangent(code[r].astype(F32), bins[r].astype(F32)))

    rows = EXT * 8
    spot = lax.broadcasted_iota(jnp.int32, (rows, C), 0) % 8

    def column(own, side):
        one = cw_corner[32 * side : 32 * side + 32, :].astype(F32)
        two = ccw_corner[32 * side : 32 * side + 32, :].astype(F32)

        def end(value, mirrored):
            tiles = [value[8 * k : 8 * k + 8] for k in range(4)]
            return jnp.where(mirrored, jnp.concatenate(tiles[::-1], axis=0), value)

        north = end(jnp.where(low, one, two), at_north)
        south = end(jnp.where(low, two, one), at_south)
        return jnp.concatenate([north, own[...].astype(F32), south], axis=0)

    left = column(from_west, 0)
    right = column(from_east, 1)

    def turned(value, by):
        return pltpu.roll(value, by % rows, 0)

    right_x = jnp.where(spot < 4, right, 0.0)
    left_x = jnp.where(spot >= 4, turned(left, 4), 0.0)
    right_q = jnp.where(spot < 2, turned(right, -4), 0.0)
    left_q = jnp.where(spot >= 6, turned(left, 2), 0.0)
    blank = jnp.zeros((8, C), F32)
    put(x32, -8, blank)
    put(x32, 0, blank)
    put(x32, N - 8, blank)
    put(x32, N, blank)
    for r in range(EXT):
        part = slice(r * 8, r * 8 + 8)
        put(x32, (r + 1) * W, right_x[part])
        put(x32, r * W + 8, left_x[part])
        if 2 <= r < 22:
            put(q32, (r + 1) * W, right_q[part])
            put(q32, r * W + 8, left_q[part])
    put(q32, 2 * W, blank)
    put(q32, 22 * W + 8, blank)

    def product(source, at, count, weights, order):
        total = None
        for slot in range(3):
            begin = order[slot]
            if not isinstance(begin, int):
                begin = pl.multiple_of(begin, 256)
            piece = jnp.dot(
                source[at + (slot - 1) * W : at + (slot - 1) * W + count, :],
                weights[pl.ds(begin, 768), :],
                preferred_element_type=F32,
            )
            total = piece if total is None else total + piece
        return total

    def returned(parts, weights, a):
        total = None
        for b in range(3):
            begin = (3 * a + 2 - b) * 256
            if not isinstance(begin, int):
                begin = pl.multiple_of(begin, 256)
            piece = lax.dot_general(
                parts[:, 256 * b : 256 * (b + 1)],
                weights[pl.ds(begin, 256), :],
                (((1,), (1,)), ((), ())),
                preferred_element_type=F32,
            )
            total = piece if total is None else total + piece
        return total

    plain = (0, 768, 1536)
    top_flip = (jnp.where(at_north, 1536, 0), 768, jnp.where(at_north, 0, 1536))
    low_flip = (jnp.where(at_south, 1536, 0), 768, jnp.where(at_south, 0, 1536))
    above_tap = jnp.where(at_north, 0, 2)
    below_tap = jnp.where(at_south, 2, 0)

    def pieces(first, last, top, bottom, orders, plain=plain):
        cuts = [(first, top, orders[0])]
        middle = (bottom - top) // 2
        cuts += [(top, top + middle, plain), (top + middle, bottom, plain)]
        cuts += [(bottom, last, orders[1])]
        out = []
        for i, (start, stop, order) in enumerate(cuts):
            out.append((start * W, (stop - start) * W + 16, 8 if i else 0, order))
        return out

    spread(lat3, x32, 0, N)
    fetches[3].wait()
    for at, count, skip, order in pieces(1, 23, 4, 20, (top_flip, low_flip)):
        pre = product(lat3, at, count, w1, order)[skip:]
        sig = jax.nn.sigmoid(pre)
        put(dact, at + skip, sig * (1.0 + pre * (1.0 - sig)))
        put(a32, at + skip, pre * sig)

    spread(act3, a32, W, 23 * W + 16)
    fetches[12].wait()
    for at, count, skip, order in pieces(2, 22, 4, 20, (top_flip, low_flip)):
        conv = product(act3, at, count, w2, order)[skip:]
        size = count - skip
        bounded = jnp.tanh(get(x32, at + skip, size) + conv)
        out = get(q32, at + skip, size) * (1.0 - bounded * bounded)
        put(g32, at + skip, out.astype(BF16).astype(F32))

    def own_cells(source, shift):
        return jnp.concatenate(
            [source[(r + shift) * W + 16 : (r + shift) * W + 80, :] for r in range(4, 20)], axis=0
        )

    def weight_grad(source, grad3, lane):
        turn[...] = jnp.transpose(own_cells(grad3.at[:, 256:512], 0))
        for a in range(3):
            full = jnp.dot(turn[...], own_cells(source, a - 1), preferred_element_type=F32)
            full = full.reshape(8, 2, 16, 768) * (1.0 / 512.0)
            mine = jnp.where(core == 0, full[:, 0], full[:, 1])
            other = jnp.where(core == 0, full[:, 1], full[:, 0])
            keep[:, :, lane + 768 * a : lane + 768 * (a + 1)] = mine
            send[:, :, lane + 768 * a : lane + 768 * (a + 1)] = other.astype(BF16)

    spread(go3, g32, 2 * W, 22 * W + 16)
    weight_grad(act3, go3, TAPS)

    taps = ((above_tap, 1, 0), (2, 1, below_tap))
    for at, count, skip, order in pieces(3, 21, 5, 19, taps, (2, 1, 0)):
        back = None
        for slot in range(3):
            begin = at + (slot - 1) * W
            piece = returned(go3[begin : begin + count, :], w2, order[slot])
            back = piece if back is None else back + piece
        back = back[skip:]
        grad = back * get(dact, at + skip, count - skip)
        put(p32, at + skip, grad)

    spread(gp3, p32, 3 * W, 21 * W + 16)
    weight_grad(lat3, gp3, 0)

    def rows_of(first, count):
        return jnp.concatenate([gp3[r * W + 16 : r * W + 80, :] for r in range(first, first + count)], axis=0)

    def tapped(first, count, a):
        return returned(rows_of(first, count), w1, a)

    above = jnp.concatenate([tapped(3, 1, above_tap), tapped(4, 15, 2)], axis=0)
    below = jnp.concatenate([tapped(5, 15, 0), tapped(20, 1, below_tap)], axis=0)
    total = tapped(4, 16, 1) + above + below
    for r in range(ROWS):
        grad_latent[r] = total[r * COLS : (r + 1) * COLS] + get(g32, (4 + r) * W + 16, COLS)


def after_core_kernel(keep, got, own, s1, s2, s3):
    x = lax.axis_index("x")

    def part(to):
        return keep[pl.ds(2 * to, 2)] + got[pl.ds(2 * to, 2)].astype(F32)

    own[...] = part(x)
    for k, out in ((1, s1), (2, s2), (3, s3)):
        out[...] = part((x + k) % 4).astype(BF16)


def after_x_kernel(own_in, r1, r2, r3, own, s1, s2, s3, parts):
    yl, yh = lax.axis_index("yl"), lax.axis_index("yh")
    for h in range(2):
        total = own_in[h] + r1[h].astype(F32) + r2[h].astype(F32) + r3[h].astype(F32)
        for tensor in range(2):
            for odd in range(2):
                lanes = [tensor * TAPS + 144 * (2 * z + odd) for z in range(8)]
                chosen = jnp.concatenate([total[:, lane : lane + 144] for lane in lanes], axis=1)
                parts[odd, h, 16 * tensor : 16 * tensor + 16, :] = chosen
    own[...] = parts[yl, yh]
    s1[...] = parts[1 - yl, yh].astype(BF16)
    s2[...] = parts[yl, 1 - yh].astype(BF16)
    s3[...] = parts[1 - yl, 1 - yh].astype(BF16)


def after_y_kernel(own_in, r1, r2, r3, out):
    total = own_in[...] + r1[...].astype(F32) + r2[...].astype(F32) + r3[...].astype(F32)
    for z in range(8):
        out[z] = total[:, 144 * z : 144 * z + 144].astype(BF16)


def local_call(kernel, outs, scratch=(), near=True, room=8, far_ins=(), near_outs=None):
    whole = pl.BlockSpec(memory_space=pltpu.VMEM)
    far = pl.BlockSpec(memory_space=pl.ANY)

    def call(*operands):
        if near:
            operands = [pltpu.with_memory_space_constraint(v, pltpu.VMEM) for v in operands]
        shapes = [
            pltpu.VMEM(shape, kind) if near_outs is None or i in near_outs else jax.ShapeDtypeStruct(shape, kind)
            for i, (shape, kind) in enumerate(outs)
        ]
        return pl.pallas_call(
            kernel,
            out_shape=shapes,
            in_specs=[far if i in far_ins else whole for i in range(len(operands))],
            out_specs=[whole] * len(outs),
            scratch_shapes=list(scratch),
            compiler_params=pltpu.CompilerParams(vmem_limit_bytes=room * 1024 * 1024),
        )(*operands)

    return call


def summed(send, keep):
    got = lax.ppermute(send, "core", [(0, 1), (1, 0)])
    size = (2, 16, 2 * TAPS)
    own, s1, s2, s3 = local_call(after_core_kernel, [(size, F32)] + [(size, BF16)] * 3)(keep, got)
    r1, r2, r3 = [
        moved(s, lambda z, yl, x, yh, core, k=k: (z, yl, (x + k) % 4, yh, core)) for k, s in ((1, s1), (2, s2), (3, s3))
    ]
    size = (32, TAPS // 2)
    own, s1, s2, s3 = local_call(
        after_x_kernel, [(size, F32)] + [(size, BF16)] * 3, [pltpu.VMEM((2, 2) + size, F32)]
    )(own, r1, r2, r3)
    r1 = moved(s1, lambda z, yl, x, yh, core: (z, 1 - yl, x, yh, core))
    r2 = moved(s2, lambda z, yl, x, yh, core: (z, yl, x, 1 - yh, core))
    r3 = moved(s3, lambda z, yl, x, yh, core: (z, 1 - yl, x, 1 - yh, core))
    (parts,) = local_call(after_y_kernel, [((8, 32, 144), BF16)])(own, r1, r2, r3)
    parts = lax.all_to_all(parts, "z", 0, 0)
    total = jnp.sum(parts.astype(F32), axis=0)
    return total[:16].T, total[16:].T


def on_device(latent, w_first, w_second, levels, prior_scale, bins, code_grad):
    levels = levels.reshape(1, C)
    prior = prior_scale.reshape(1, C)
    given = [pltpu.with_memory_space_constraint(v, pltpu.HBM) for v in (latent, code_grad, bins, levels, prior)]
    edge = ((6, COLS, C), BF16)
    strip = ((ROWS * 8, C), BF16)
    corner = ((64, C), BF16)
    cells = (ROWS, COLS, C)
    cw, ccw, east, west = local_call(
        rims_kernel,
        [edge, edge, strip, strip],
        [pltpu.VMEM(v.shape, v.dtype) for v in given] + [pltpu.SemaphoreType.DMA((5,))],
        near=False, far_ins=range(5),
    )(*given)
    from_west = lax.ppermute(east, ("z", "yl"), [(i, (i + 1) % 16) for i in range(16)])
    from_east = lax.ppermute(west, ("z", "yl"), [((i + 1) % 16, i) for i in range(16)])
    cw = lax.ppermute(cw, FINE, ring_pairs(1))
    ccw = lax.ppermute(ccw, FINE, ring_pairs(-1))
    cw_corner, ccw_corner = local_call(corners_kernel, [corner] * 2)(from_west, from_east)
    cw_corner = lax.ppermute(cw_corner, FINE, ring_pairs(1))
    ccw_corner = lax.ppermute(ccw_corner, FINE, ring_pairs(-1))

    frame = pltpu.VMEM((2, N + 2 * BASE, 128), F32)
    triple = pltpu.VMEM((N, 3 * C), BF16)
    w1, w2 = [pltpu.with_memory_space_constraint(w.reshape(TAPS, C), pltpu.HBM) for w in (w_first, w_second)]
    fars = given[:3] + [w1, cw, ccw, from_east, from_west, cw_corner, ccw_corner] + given[3:] + [w2]
    grad_latent, send, keep = local_call(
        block_kernel,
        [(cells, F32), ((8, 16, 2 * TAPS), BF16), ((8, 16, 2 * TAPS), F32)],
        [pltpu.VMEM(v.shape, v.dtype) for v in fars]
        + [frame] * 5 + [triple] * 4 + [pltpu.VMEM((C, ROWS * COLS), BF16), pltpu.SemaphoreType.DMA((13,))],
        near=False, room=44, far_ins=range(13), near_outs=(1, 2),
    )(*fars)
    grad_first, grad_second = summed(send, keep)
    return (grad_latent, grad_first, grad_second)


def solution(mesh):
    fine = Mesh(mesh.devices.reshape(8, 2, 4, 2, 2), FINE)
    lon, lat = ("z", "yl"), ("x", "yh", "core")
    placed = (P(lat, lon, None), P(), P(), P(), P(), P(lat, lon, None), P(lat, lon, None))
    return jax.shard_map(
        on_device,
        mesh=fine,
        in_specs=placed,
        out_specs=(P(lat, lon, None), P(lon, lat), P(lon, lat)),
        check_vma=False,
    )
```

```python
import jax
import jax.numpy as jnp
from jax import lax
from jax.experimental import pallas as pl
from jax.experimental.pallas import tpu as pltpu
from jax.sharding import Mesh
from jax.sharding import PartitionSpec as P

RATE_WEIGHT = 0.5

F32 = jnp.float32
BF16 = jnp.bfloat16

C = 256
ROWS = 16
COLS = 64
RIM = 4
EXT = ROWS + 2 * RIM
W = 80
N = EXT * W + 16
BASE = 8
TAPS = 2304


def place():
    lon = 2 * lax.axis_index("z") + lax.axis_index("yl")
    lat = 4 * lax.axis_index("x") + 2 * lax.axis_index("yh") + lax.axis_index("core")
    return lon, lat


FINE = ("z", "yl", "x", "yh", "core")


def ring_pairs(step):
    pairs = []
    for lon in range(8):
        circle = [(lon, lat) for lat in range(16)] + [(lon + 8, lat) for lat in reversed(range(16))]
        for i, (lo, la) in enumerate(circle):
            tlo, tla = circle[(i + step) % 32]
            pairs.append((lo * 16 + la, tlo * 16 + tla))
    return pairs


def moved(block, route):
    pairs = []
    for lon in range(16):
        for lat in range(16):
            z, yl, x, yh, core = route(lon // 2, lon % 2, lat // 4, lat // 2 % 2, lat % 2)
            pairs.append((lon * 16 + lat, (z * 2 + yl) * 16 + x * 4 + yh * 2 + core))
    return lax.ppermute(block, FINE, pairs)


def cotangent_of(levels, prior):
    half_levels = (levels[...].astype(F32) - 1.0) / 2.0
    scale = prior[...]
    double = 2.0 * scale
    weight = RATE_WEIGHT * half_levels

    def cotangent(code_part, bins_part):
        slope = jnp.tanh((bins_part - half_levels) / double) / scale
        return code_part + weight * slope

    return cotangent


def fetched(pairs, arrived):
    copies = [pltpu.make_async_copy(far, near, arrived.at[i]) for i, (far, near) in enumerate(pairs)]
    for copy in copies:
        copy.start()
    return copies


def rims_kernel(
    latent_far, code_far, bins_far, levels_far, prior_far,
    cw, ccw, east, west,
    latent, code, bins, levels, prior, arrived,
):
    pairs = (
        (latent_far, latent), (code_far, code), (bins_far, bins), (levels_far, levels), (prior_far, prior),
    )
    for copy in fetched(pairs, arrived):
        copy.wait()
    lon, lat = place()
    low = lon < 8
    cotangent = cotangent_of(levels, prior)

    def outward(k, first, last):
        cw[COLS * k : COLS * (k + 1), :] = jnp.where(low, last, first).astype(BF16)
        ccw[COLS * k : COLS * (k + 1), :] = jnp.where(low, first, last).astype(BF16)

    for k in range(4):
        outward(k, latent[k].astype(F32), latent[12 + k].astype(F32))
    for k in range(2):
        outward(
            4 + k,
            cotangent(code[k].astype(F32), bins[k].astype(F32)),
            cotangent(code[14 + k].astype(F32), bins[14 + k].astype(F32)),
        )

    spot = lax.broadcasted_iota(jnp.int32, (ROWS * 8, C), 0) % 8
    for out, right in ((east, True), (west, False)):
        tile = slice(48, 64) if right else slice(0, 16)
        side = slice(8, 16) if right else slice(0, 8)
        x = latent[:, tile, :].astype(F32)[:, side].reshape(ROWS * 8, C)
        q = cotangent(
            code[:, tile, :].astype(F32)[:, side].reshape(ROWS * 8, C),
            bins[:, tile, :].astype(F32)[:, side].reshape(ROWS * 8, C),
        )
        if right:
            x = pltpu.roll(x, ROWS * 8 - 4, 0)
            q = pltpu.roll(q, ROWS * 8 - 2, 0)
        else:
            q = pltpu.roll(q, 4, 0)
        out[...] = jnp.where(spot < 4, x, q).astype(BF16)


def corners_kernel(from_west, from_east, cw_rows, ccw_rows, cw, ccw):
    lon, lat = place()
    low = lon < 8
    cw[0:384, :] = cw_rows[...]
    ccw[0:384, :] = ccw_rows[...]
    for side, strip in enumerate((from_west, from_east)):
        at = 384 + 32 * side
        first, last = strip[0:32, :].astype(F32), strip[96:128, :].astype(F32)
        cw[at : at + 32, :] = jnp.where(low, last, first).astype(BF16)
        ccw[at : at + 32, :] = jnp.where(low, first, last).astype(BF16)


def facing(first, second, low, rows, count, mirrored):
    picked = []
    for k in range(count):
        at = pl.multiple_of((rows + jnp.where(mirrored, count - 1 - k, k)) * COLS, COLS)
        one, two = first[pl.ds(at, COLS), :], second[pl.ds(at, COLS), :]
        picked.append(jnp.where(low, one.astype(F32), two.astype(F32)))
    return picked


def put(ref, at, value):
    rows = value.shape[0]
    ref[0, BASE + at : BASE + at + rows, :] = value[:, :128]
    ref[1, BASE + at : BASE + at + rows, :] = value[:, 128:]


def get(ref, at, rows):
    return jnp.concatenate([ref[0, BASE + at : BASE + at + rows, :], ref[1, BASE + at : BASE + at + rows, :]], axis=1)


def spread(dest, ref, start, stop):
    for at in range(start, stop, 320):
        rows = min(320, stop - at)
        for b in range(3):
            for half in range(2):
                lane = b * 256 + half * 128
                dest[at : at + rows, lane : lane + 128] = ref[half, pl.ds(BASE + at + b - 1, rows), :].astype(BF16)


def block_kernel(*refs):
    fars = refs[:11]
    grad_latent, send, keep = refs[11:14]
    nears = refs[14:25]
    x32, q32, a32, g32, dact, lat3, act3, go3, gp3, turn, arrived = refs[25:]
    fetches = fetched(tuple(zip(fars, nears)), arrived)
    latent, code, bins, w1, cw, ccw, from_east, from_west, levels, prior, w2 = nears
    p32 = a32
    for fetch in fetches[:3] + fetches[4:10]:
        fetch.wait()
    lon, lat = place()
    low = lon < 8
    at_north = lat == 0
    at_south = lat == 15
    core = lat % 2
    cotangent = cotangent_of(levels, prior)

    north = facing(cw, ccw, low, 0, 4, at_north)
    south = facing(ccw, cw, low, 0, 4, at_south)
    for k in range(4):
        put(x32, k * W + 16, north[k])
        put(x32, (20 + k) * W + 16, south[k])
    for r in range(ROWS):
        put(x32, (4 + r) * W + 16, latent[r].astype(F32))
    north_q = facing(cw, ccw, low, 4, 2, at_north)
    south_q = facing(ccw, cw, low, 4, 2, at_south)
    for k in range(2):
        put(q32, (2 + k) * W + 16, north_q[k])
        put(q32, (20 + k) * W + 16, south_q[k])
    for r in range(ROWS):
        put(q32, (4 + r) * W + 16, cotangent(code[r].astype(F32), bins[r].astype(F32)))

    rows = EXT * 8
    spot = lax.broadcasted_iota(jnp.int32, (rows, C), 0) % 8

    def column(own, side):
        at = 384 + 32 * side
        one, two = cw[at : at + 32, :].astype(F32), ccw[at : at + 32, :].astype(F32)

        def end(value, mirrored):
            tiles = [value[8 * k : 8 * k + 8] for k in range(4)]
            return jnp.where(mirrored, jnp.concatenate(tiles[::-1], axis=0), value)

        north = end(jnp.where(low, one, two), at_north)
        south = end(jnp.where(low, two, one), at_south)
        return jnp.concatenate([north, own[...].astype(F32), south], axis=0)

    left = column(from_west, 0)
    right = column(from_east, 1)

    def turned(value, by):
        return pltpu.roll(value, by % rows, 0)

    right_x = jnp.where(spot < 4, right, 0.0)
    left_x = jnp.where(spot >= 4, turned(left, 4), 0.0)
    right_q = jnp.where(spot < 2, turned(right, -4), 0.0)
    left_q = jnp.where(spot >= 6, turned(left, 2), 0.0)
    blank = jnp.zeros((8, C), F32)
    put(x32, -8, blank)
    put(x32, 0, blank)
    put(x32, N - 8, blank)
    put(x32, N, blank)
    for r in range(EXT):
        part = slice(r * 8, r * 8 + 8)
        put(x32, (r + 1) * W, right_x[part])
        put(x32, r * W + 8, left_x[part])
        if 2 <= r < 22:
            put(q32, (r + 1) * W, right_q[part])
            put(q32, r * W + 8, left_q[part])
    put(q32, 2 * W, blank)
    put(q32, 22 * W + 8, blank)

    def product(source, at, count, weights, order):
        total = None
        for slot in range(3):
            begin = order[slot]
            if not isinstance(begin, int):
                begin = pl.multiple_of(begin, 256)
            piece = jnp.dot(
                source[at + (slot - 1) * W : at + (slot - 1) * W + count, :],
                weights[pl.ds(begin, 768), :],
                preferred_element_type=F32,
            )
            total = piece if total is None else total + piece
        return total

    def returned(parts, weights, a):
        total = None
        for b in range(3):
            begin = (3 * a + 2 - b) * 256
            if not isinstance(begin, int):
                begin = pl.multiple_of(begin, 256)
            piece = lax.dot_general(
                parts[:, 256 * b : 256 * (b + 1)],
                weights[pl.ds(begin, 256), :],
                (((1,), (1,)), ((), ())),
                preferred_element_type=F32,
            )
            total = piece if total is None else total + piece
        return total

    plain = (0, 768, 1536)
    top_flip = (jnp.where(at_north, 1536, 0), 768, jnp.where(at_north, 0, 1536))
    low_flip = (jnp.where(at_south, 1536, 0), 768, jnp.where(at_south, 0, 1536))
    above_tap = jnp.where(at_north, 0, 2)
    below_tap = jnp.where(at_south, 2, 0)

    def pieces(first, last, top, bottom, orders, plain=plain):
        cuts = [(first, top, orders[0])]
        middle = (bottom - top) // 2
        cuts += [(top, top + middle, plain), (top + middle, bottom, plain)]
        cuts += [(bottom, last, orders[1])]
        out = []
        for i, (start, stop, order) in enumerate(cuts):
            out.append((start * W, (stop - start) * W + 16, 8 if i else 0, order))
        return out

    spread(lat3, x32, 0, N)
    fetches[3].wait()
    for at, count, skip, order in pieces(1, 23, 4, 20, (top_flip, low_flip)):
        pre = product(lat3, at, count, w1, order)[skip:]
        sig = jax.nn.sigmoid(pre)
        put(dact, at + skip, sig * (1.0 + pre * (1.0 - sig)))
        put(a32, at + skip, pre * sig)

    spread(act3, a32, W, 23 * W + 16)
    fetches[10].wait()
    for at, count, skip, order in pieces(2, 22, 4, 20, (top_flip, low_flip)):
        conv = product(act3, at, count, w2, order)[skip:]
        size = count - skip
        bounded = jnp.tanh(get(x32, at + skip, size) + conv)
        out = get(q32, at + skip, size) * (1.0 - bounded * bounded)
        put(g32, at + skip, out.astype(BF16).astype(F32))

    def own_cells(source, shift):
        return jnp.concatenate(
            [source[(r + shift) * W + 16 : (r + shift) * W + 80, :] for r in range(4, 20)], axis=0
        )

    def weight_grad(source, grad3, lane):
        turn[...] = jnp.transpose(own_cells(grad3.at[:, 256:512], 0))
        for a in range(3):
            full = jnp.dot(turn[...], own_cells(source, a - 1), preferred_element_type=F32)
            full = full.reshape(8, 2, 16, 768) * (1.0 / 512.0)
            mine = jnp.where(core == 0, full[:, 0], full[:, 1])
            other = jnp.where(core == 0, full[:, 1], full[:, 0])
            keep[:, :, lane + 768 * a : lane + 768 * (a + 1)] = mine
            send[:, :, lane + 768 * a : lane + 768 * (a + 1)] = other.astype(BF16)

    spread(go3, g32, 2 * W, 22 * W + 16)
    weight_grad(act3, go3, TAPS)

    taps = ((above_tap, 1, 0), (2, 1, below_tap))
    for at, count, skip, order in pieces(3, 21, 5, 19, taps, (2, 1, 0)):
        back = None
        for slot in range(3):
            begin = at + (slot - 1) * W
            piece = returned(go3[begin : begin + count, :], w2, order[slot])
            back = piece if back is None else back + piece
        back = back[skip:]
        grad = back * get(dact, at + skip, count - skip)
        put(p32, at + skip, grad)

    spread(gp3, p32, 3 * W, 21 * W + 16)
    weight_grad(lat3, gp3, 0)

    def rows_of(first, count):
        return jnp.concatenate([gp3[r * W + 16 : r * W + 80, :] for r in range(first, first + count)], axis=0)

    def tapped(first, count, a):
        return returned(rows_of(first, count), w1, a)

    above = jnp.concatenate([tapped(3, 1, above_tap), tapped(4, 15, 2)], axis=0)
    below = jnp.concatenate([tapped(5, 15, 0), tapped(20, 1, below_tap)], axis=0)
    total = tapped(4, 16, 1) + above + below
    for r in range(ROWS):
        grad_latent[r] = total[r * COLS : (r + 1) * COLS] + get(g32, (4 + r) * W + 16, COLS)


def after_core_kernel(keep, got, own, s1, s2, s3):
    x = lax.axis_index("x")

    def part(to):
        return keep[pl.ds(2 * to, 2)] + got[pl.ds(2 * to, 2)].astype(F32)

    own[...] = part(x)
    for k, out in ((1, s1), (2, s2), (3, s3)):
        out[...] = part((x + k) % 4).astype(BF16)


def after_x_kernel(own_in, r1, r2, r3, own, s1, s2, s3, parts):
    yl, yh = lax.axis_index("yl"), lax.axis_index("yh")
    for h in range(2):
        total = own_in[h] + r1[h].astype(F32) + r2[h].astype(F32) + r3[h].astype(F32)
        for tensor in range(2):
            for odd in range(2):
                lanes = [tensor * TAPS + 144 * (2 * z + odd) for z in range(8)]
                chosen = jnp.concatenate([total[:, lane : lane + 144] for lane in lanes], axis=1)
                parts[odd, h, 16 * tensor : 16 * tensor + 16, :] = chosen
    own[...] = parts[yl, yh]
    s1[...] = parts[1 - yl, yh].astype(BF16)
    s2[...] = parts[yl, 1 - yh].astype(BF16)
    s3[...] = parts[1 - yl, 1 - yh].astype(BF16)


def after_y_kernel(own_in, r1, r2, r3, out):
    total = own_in[...] + r1[...].astype(F32) + r2[...].astype(F32) + r3[...].astype(F32)
    for z in range(8):
        out[z] = total[:, 144 * z : 144 * z + 144].astype(BF16)


def local_call(kernel, outs, scratch=(), near=True, room=8, far_ins=(), near_outs=None):
    whole = pl.BlockSpec(memory_space=pltpu.VMEM)
    far = pl.BlockSpec(memory_space=pl.ANY)

    def call(*operands):
        if near:
            operands = [pltpu.with_memory_space_constraint(v, pltpu.VMEM) for v in operands]
        shapes = [
            pltpu.VMEM(shape, kind) if near_outs is None or i in near_outs else jax.ShapeDtypeStruct(shape, kind)
            for i, (shape, kind) in enumerate(outs)
        ]
        return pl.pallas_call(
            kernel,
            out_shape=shapes,
            in_specs=[far if i in far_ins else whole for i in range(len(operands))],
            out_specs=[whole] * len(outs),
            scratch_shapes=list(scratch),
            compiler_params=pltpu.CompilerParams(vmem_limit_bytes=room * 1024 * 1024),
        )(*operands)

    return call


def summed(send, keep):
    got = lax.ppermute(send, "core", [(0, 1), (1, 0)])
    size = (2, 16, 2 * TAPS)
    own, s1, s2, s3 = local_call(after_core_kernel, [(size, F32)] + [(size, BF16)] * 3)(keep, got)
    r1, r2, r3 = [
        moved(s, lambda z, yl, x, yh, core, k=k: (z, yl, (x + k) % 4, yh, core)) for k, s in ((1, s1), (2, s2), (3, s3))
    ]
    size = (32, TAPS // 2)
    own, s1, s2, s3 = local_call(
        after_x_kernel, [(size, F32)] + [(size, BF16)] * 3, [pltpu.VMEM((2, 2) + size, F32)]
    )(own, r1, r2, r3)
    r1 = moved(s1, lambda z, yl, x, yh, core: (z, 1 - yl, x, yh, core))
    r2 = moved(s2, lambda z, yl, x, yh, core: (z, yl, x, 1 - yh, core))
    r3 = moved(s3, lambda z, yl, x, yh, core: (z, 1 - yl, x, 1 - yh, core))
    (parts,) = local_call(after_y_kernel, [((8, 32, 144), BF16)])(own, r1, r2, r3)
    parts = lax.all_to_all(parts, "z", 0, 0)
    total = jnp.sum(parts.astype(F32), axis=0)
    return total[:16].T, total[16:].T


def on_device(latent, w_first, w_second, levels, prior_scale, bins, code_grad):
    levels = levels.reshape(1, C)
    prior = prior_scale.reshape(1, C)
    given = [pltpu.with_memory_space_constraint(v, pltpu.HBM) for v in (latent, code_grad, bins, levels, prior)]
    edge = ((6 * COLS, C), BF16)
    strip = ((ROWS * 8, C), BF16)
    message = ((6 * COLS + 64, C), BF16)
    cells = (ROWS, COLS, C)
    cw, ccw, east, west = local_call(
        rims_kernel,
        [edge, edge, strip, strip],
        [pltpu.VMEM(v.shape, v.dtype) for v in given] + [pltpu.SemaphoreType.DMA((5,))],
        near=False, far_ins=range(5),
    )(*given)
    from_west = lax.ppermute(east, ("z", "yl"), [(i, (i + 1) % 16) for i in range(16)])
    from_east = lax.ppermute(west, ("z", "yl"), [((i + 1) % 16, i) for i in range(16)])
    cw, ccw = local_call(corners_kernel, [message] * 2)(from_west, from_east, cw, ccw)
    cw = lax.ppermute(cw, FINE, ring_pairs(1))
    ccw = lax.ppermute(ccw, FINE, ring_pairs(-1))

    frame = pltpu.VMEM((2, N + 2 * BASE, 128), F32)
    triple = pltpu.VMEM((N, 3 * C), BF16)
    w1, w2 = [pltpu.with_memory_space_constraint(w.reshape(TAPS, C), pltpu.HBM) for w in (w_first, w_second)]
    fars = given[:3] + [w1, cw, ccw, from_east, from_west] + given[3:] + [w2]
    grad_latent, send, keep = local_call(
        block_kernel,
        [(cells, F32), ((8, 16, 2 * TAPS), BF16), ((8, 16, 2 * TAPS), F32)],
        [pltpu.VMEM(v.shape, v.dtype) for v in fars]
        + [frame] * 5 + [triple] * 4 + [pltpu.VMEM((C, ROWS * COLS), BF16), pltpu.SemaphoreType.DMA((11,))],
        near=False, room=44, far_ins=range(11), near_outs=(1, 2),
    )(*fars)
    grad_first, grad_second = summed(send, keep)
    return (grad_latent, grad_first, grad_second)


def solution(mesh):
    fine = Mesh(mesh.devices.reshape(8, 2, 4, 2, 2), FINE)
    lon, lat = ("z", "yl"), ("x", "yh", "core")
    placed = (P(lat, lon, None), P(), P(), P(), P(), P(lat, lon, None), P(lat, lon, None))
    return jax.shard_map(
        on_device,
        mesh=fine,
        in_specs=placed,
        out_specs=(P(lat, lon, None), P(lon, lat), P(lon, lat)),
        check_vma=False,
    )
```
